512 devices in a mesh: region: 16 (over y, x), member: 32 (over z, core).
Axes of the slice: x: 4, y: 4, z: 16, core: 2. Of those that a mesh axis runs over, the one named last changes fastest.
Arguments:
- sample_matrix: bfloat16 [128, 1048576], P('member', 'region'), may hold values from -6 to 6
- state_coords: float32 [3, 1048576], P(None, ('region', 'member')), may hold values from 0 to 1
- obs_model: bfloat16 [128, 16384], P('member', 'region'), may hold values from -6 to 6
- innovations: bfloat16 [128, 16384], P('member', 'region'), may hold values from -6 to 6
- obs_error: float32 [16384], P('region'), may hold values from 0.25 to 4
- obs_coords: float32 [3, 16384], P(None, 'region'), may hold values from 0 to 1
- neighbours: int32 [16, 2], P('region'), may hold values from 0 to 15, as said below
- pattern: int32 [8192, 12], P(('region', 'member')), may hold values from 0 to 23
- counts: int32 [8192], P(('region', 'member')), may hold values from 1 to 12
Outputs:
- analysis: bfloat16 [128, 1048576], P('member', 'region')
The draws below stay inside these ranges and needn't reach their ends.
Inputs may be any that keep to these rules, and one draw needn't show every extreme that they name: `neighbours`: two distinct regions, both other than the region itself.
All inputs are finite; a program needn't handle non-finite values.
Results may differ from the reference program's by a relative error of at most 0.011.
Values may be sent and summed in bfloat16 or wider, within the bound.
A program may use at most 64 MiB of HBM per device.

```python
import math
import jax
import jax.numpy as jnp
from jax import lax

MEMBERS = 128
TILE_SIZE = 128
SB_DEV = 16
OB_REG = 8
PAT = 12
REGIONS = 16
SB_REG = 512
TILE_NUMBER = 8192
ENTRIES = 1048576
OBS = 16384
PANELS = 24


def draw_neighbours(key, part):
    key = jax.random.fold_in(key, 11)
    first_key = jax.random.fold_in(key, 1)
    second_key = jax.random.fold_in(key, 2)
    regions_all = jnp.arange(REGIONS, dtype=jnp.int32)
    first_offset = jax.random.randint(first_key, (REGIONS,), 1, REGIONS, dtype=jnp.int32)
    second_raw = jax.random.randint(second_key, (REGIONS,), 1, REGIONS - 1, dtype=jnp.int32)
    second_offset = jnp.where(second_raw >= first_offset, second_raw + 1, second_raw)
    first_region = (regions_all + first_offset) % REGIONS
    second_region = (regions_all + second_offset) % REGIONS
    return jnp.stack([first_region, second_region], axis=1).astype(jnp.int32)


def draw_counts(key, part):
    key = jax.random.fold_in(key, 23)
    cap_key = jax.random.fold_in(key, 1)
    count_key = jax.random.fold_in(key, 2)
    region_cap = jax.random.randint(cap_key, (REGIONS,), max(1, PAT // 4), PAT + 1, dtype=jnp.int32)
    region_cap = region_cap.at[0].set(PAT)
    region_of = jnp.arange(TILE_NUMBER, dtype=jnp.int32) // SB_REG
    drawn = jax.random.randint(count_key, (TILE_NUMBER,), 1, region_cap[region_of] + 1, dtype=jnp.int32)
    return drawn.at[0].set(PAT).astype(jnp.int32)


def with_ends(array, key, smallest, high):
    dims = array.shape
    index_at = [jax.random.randint(jax.random.fold_in(key, axis), (), 0, dims[axis]) for axis in range(len(dims))]
    array = array.at[tuple(index_at)].set(smallest)
    longest = dims.index(max(dims))
    index_at[longest] = (index_at[longest] + 1) % dims[longest]
    return array.at[tuple(index_at)].set(high)


def steps_of(own_key, shape, cuts, least, top_value):
    level, own = 1.0, jax.random.fold_in(own_key, 6)
    for axis_at, parts in cuts:
        draws = jnp.exp(jax.random.uniform(jax.random.fold_in(own, axis_at), (parts,), jnp.float32, least / len(cuts), top_value / len(cuts)))
        level = level * jnp.repeat(draws, shape[axis_at] // parts).reshape([-1 if axis == axis_at else 1 for axis in range(len(shape))])
    return level


def gaussian(rng, dims, scale, most, pieces=(), kind=jnp.bfloat16):
    array = jax.random.normal(rng, dims, jnp.float32) * scale
    if len(pieces) > 0:
        array = steps_of(rng, dims, pieces, -0.22, 0.18) * array
    return jnp.clip(array, min=-most, max=most).astype(kind)


def setup_inputs(seed: int = 0) -> dict:
    arg_keys = jax.random.split(jax.random.key(seed), 10)
    return {
        "sample_matrix": gaussian(arg_keys[0], (MEMBERS, ENTRIES), 1.0, 6.0, ((0, 32), (1, 16))),
        "state_coords": jnp.clip(1.0 * jax.random.uniform(arg_keys[1], (3, ENTRIES), jnp.float32) ** steps_of(arg_keys[1], (3, ENTRIES), ((1, 512),), -0.2, 0.2), 0.0, 1.0),
        "obs_model": gaussian(arg_keys[2], (MEMBERS, OBS), 1.0, 6.0, ((0, 32), (1, 16))),
        "innovations": gaussian(arg_keys[3], (MEMBERS, OBS), 1.0, 6.0, ((0, 32), (1, 16))),
        "obs_error": jnp.clip(jnp.exp(math.log(4.0) - 2.7725887 * jax.random.uniform(arg_keys[4], (OBS,), jnp.float32) ** steps_of(arg_keys[4], (OBS,), ((0, 16),), -0.2, 0.2)), 0.25, 4.0),
        "obs_coords": jnp.clip(1.0 * jax.random.uniform(arg_keys[5], (3, OBS), jnp.float32) ** steps_of(arg_keys[5], (3, OBS), ((1, 16),), -0.2, 0.2), 0.0, 1.0),
        "neighbours": draw_neighbours(jax.random.fold_in(arg_keys[9], 71), 0),
        "pattern": with_ends(jax.random.randint(arg_keys[7], (TILE_NUMBER, PAT), 0, PANELS), jax.random.fold_in(arg_keys[7], 1), 0, PANELS - 1).astype(jnp.int32),
        "counts": draw_counts(jax.random.fold_in(arg_keys[9], 71), 0),
    }


half_width = 0.6

def gaspari(distance):
    scaled = distance / half_width
    near_part = (((-0.25 * scaled + 0.5) * scaled + 0.625) * scaled - 5.0 / 3.0) * scaled * scaled + 1.0
    clipped = jnp.maximum(scaled, 1.0)
    far_part = ((((scaled / 12.0 - 0.5) * scaled + 0.625) * scaled + 5.0 / 3.0) * scaled - 5.0) * scaled + 4.0 - 2.0 / (3.0 * clipped)
    return jnp.where(scaled <= 1.0, near_part, jnp.where(scaled <= 2.0, far_part, 0.0))

def reference(sample_matrix, state_coords, obs_model, innovations, obs_error, obs_coords, neighbours, pattern, counts):
    sample_collection = MEMBERS
    state_float = sample_matrix.astype(jnp.float32)
    centre = lax.optimization_barrier(jnp.sum(state_float, axis=0)) / sample_collection
    state_anom = (state_float - centre).astype(jnp.bfloat16).reshape(sample_collection, TILE_NUMBER, TILE_SIZE)
    model_float = obs_model.astype(jnp.float32)
    obs_dev = model_float - lax.optimization_barrier(jnp.sum(model_float, axis=0)) / sample_collection
    spread = lax.optimization_barrier(jnp.sum(obs_dev * obs_dev, axis=0)) / (sample_collection - 1) + obs_error
    obs_anom = obs_dev.astype(jnp.bfloat16).reshape(sample_collection, REGIONS * OB_REG, TILE_SIZE)
    weighted = (innovations.astype(jnp.float32) / spread).astype(jnp.bfloat16).reshape(sample_collection, REGIONS * OB_REG, TILE_SIZE)
    obs_xyz = obs_coords.reshape(3, REGIONS * OB_REG, TILE_SIZE)
    state_xyz = state_coords.reshape(3, TILE_NUMBER, TILE_SIZE)
    region_of = (jnp.arange(TILE_NUMBER) // SB_REG).astype(jnp.int32)
    region_table = jnp.concatenate([jnp.arange(REGIONS, dtype=jnp.int32)[:, None], neighbours.astype(jnp.int32)], axis=1)
    panel_slot = pattern // OB_REG
    owner_region = region_table[region_of[:, None], panel_slot]
    global_ids = (owner_region * OB_REG + pattern % OB_REG).astype(jnp.int32)
    live_mask = (jnp.arange(PAT)[None, :] < counts[:, None]).astype(jnp.float32)
    batch_extent = SB_DEV

    def one_group(group_index):
        opening_tile = (group_index * batch_extent).astype(jnp.int32)
        state_dev = lax.dynamic_slice_in_dim(state_anom, opening_tile, batch_extent, 1).astype(jnp.float32)
        state_pos = lax.dynamic_slice_in_dim(state_xyz, opening_tile, batch_extent, 1)
        background_sample = lax.dynamic_slice_in_dim(sample_matrix.reshape(sample_collection, TILE_NUMBER, TILE_SIZE), opening_tile, batch_extent, 1)
        slot_ids = lax.dynamic_slice_in_dim(global_ids, opening_tile, batch_extent, 0).reshape(-1)
        group_live = lax.dynamic_slice_in_dim(live_mask, opening_tile, batch_extent, 0)
        obs_part = jnp.take(obs_anom, slot_ids, axis=1).reshape(sample_collection, batch_extent, PAT, TILE_SIZE).astype(jnp.float32)
        obs_weight = jnp.take(weighted, slot_ids, axis=1).reshape(sample_collection, batch_extent, PAT, TILE_SIZE).astype(jnp.float32)
        obs_pos = jnp.take(obs_xyz, slot_ids, axis=1).reshape(3, batch_extent, PAT, TILE_SIZE)
        covariance = jnp.einsum('mbe,mbjo->bjeo', state_dev, obs_part) / (sample_collection - 1)
        offset = state_pos[:, :, None, :, None] - obs_pos[:, :, :, None, :]
        distance = jnp.sqrt(offset[0] * offset[0] + offset[1] * offset[1] + offset[2] * offset[2])
        gain_block = (gaspari(distance) * covariance * group_live[:, :, None, None]).astype(jnp.bfloat16)
        update_shift = jnp.einsum('mbjo,bjeo->mbe', obs_weight, gain_block.astype(jnp.float32))
        return (background_sample.astype(jnp.float32) + update_shift).astype(jnp.bfloat16)
    updated = lax.map(one_group, jnp.arange(TILE_NUMBER // batch_extent, dtype=jnp.int32))
    return jnp.transpose(updated, (1, 0, 2, 3)).reshape(sample_collection, ENTRIES)
```

```python
import functools

import jax
import jax.numpy as jnp
from jax import lax
from jax.experimental import pallas as pl
from jax.experimental.pallas import tpu as pltpu
from jax.sharding import PartitionSpec as P

MESH = pl.DeviceIdType.MESH
F32 = jnp.float32
BF16 = jnp.bfloat16
TILE = 128
FEATS = 32
HALF_WIDTH = 0.6
CHUNKS = 4


def split3(v):
    first = v.astype(BF16).astype(F32)
    rest = v - first
    second = rest.astype(BF16).astype(F32)
    third = (rest - second).astype(BF16).astype(F32)
    return first, second, third


def pieces(coords):
    row = lax.broadcasted_iota(jnp.int32, coords.shape, 0)
    scaled = jnp.where(row < 3, (coords - 0.5) * (1.0 / HALF_WIDTH), 0.0)
    norm = jnp.sum(scaled * scaled, axis=0, keepdims=True)
    n1, n2, n3 = split3(norm)
    norms = jnp.where(row == 0, n1, jnp.where(row == 1, n2, jnp.where(row == 2, n3, 0.0)))
    ones = jnp.where(row < 3, 1.0, 0.0)
    return split3(scaled), norms, ones


def taper(square, scale):
    square = jnp.maximum(square, 1e-12)
    inverse = lax.rsqrt(square)
    z = square * inverse
    near = (
        ((-0.25 * scale * z + 0.5 * scale) * z + 0.625 * scale) * z - 5.0 / 3.0 * scale
    ) * square + scale
    edge = jnp.maximum(2.0 - z, 0.0)
    edge = edge * edge
    far = (edge * edge) * ((scale / 12.0) * z + (scale / 6.0) - (scale / 24.0) * inverse)
    return jnp.where(square <= 1.0, near, far)


def kernel(
    dims,
    sample,
    obs,
    innov,
    error,
    obs_coords,
    state_coords,
    neighbours,
    pattern,
    counts,
    out,
    mine,
    geo,
    gathered,
    gathered_geo,
    ring,
    geo_sel,
    arrived,
    fields,
    results,
    leaving,
    obs_rows,
    innov_rows,
    feat_rows,
    state_feats,
    panel_left,
    panel_weight,
    right,
    gains,
    xy_send,
    xy_recv,
    geo_send,
    geo_recv,
    up_send,
    up_recv,
    down_send,
    down_recv,
    sib_send,
    sib_recv,
    in_send,
    in_recv,
    in_own,
    out_send,
    out_recv,
):
    regions, devices = dims
    chips = devices // 2
    rows = sample.shape[0]
    members = rows * devices
    chunks, _, _, width = arrived.shape
    entries = chunks * width
    blocks = width // TILE
    slots = pattern.shape[1]
    panels = obs.shape[1] // TILE
    my_region = lax.axis_index("region")
    me = lax.axis_index("member")
    my_z = me // 2
    my_core = me % 2

    barrier = pltpu.get_barrier_semaphore()

    def greet_region(step, carry):
        peer = (my_region + step) % regions
        pl.semaphore_signal(barrier, inc=1, device_id=(peer, me), device_id_type=MESH)
        return carry

    def greet_member(step, carry):
        peer = (me + step) % devices
        pl.semaphore_signal(barrier, inc=1, device_id=(my_region, peer), device_id_type=MESH)
        return carry

    lax.fori_loop(1, regions, greet_region, 0)
    lax.fori_loop(1, devices, greet_member, 0)
    mine[0] = obs[...]
    mine[1] = innov[...]
    geo[0:3, :] = obs_coords[...]
    geo[3:4, :] = error[...]
    gathered[my_region] = mine[...]
    gathered_geo[my_region] = geo[...]
    pl.semaphore_wait(barrier, regions + devices - 2)

    def send_region(step, carry):
        peer = (my_region + step) % regions
        pltpu.make_async_remote_copy(
            src_ref=mine,
            dst_ref=gathered.at[my_region],
            send_sem=xy_send,
            recv_sem=xy_recv,
            device_id=(peer, me),
            device_id_type=MESH,
        ).start()
        pltpu.make_async_remote_copy(
            src_ref=geo,
            dst_ref=gathered_geo.at[my_region],
            send_sem=geo_send,
            recv_sem=geo_recv,
            device_id=(peer, me),
            device_id_type=MESH,
        ).start()
        return carry

    lax.fori_loop(1, regions, send_region, 0)

    def send_samples(chunk):
        def send(step, carry):
            peer = (me + step) % devices
            begin = pl.multiple_of(peer * entries + chunk * width, TILE)
            pltpu.make_async_remote_copy(
                src_ref=sample.at[:, pl.ds(begin, width)],
                dst_ref=arrived.at[chunk, me],
                send_sem=in_send,
                recv_sem=in_recv.at[chunk],
                device_id=(my_region, peer),
                device_id_type=MESH,
            ).start()
            return carry

        lax.fori_loop(1, devices, send, 0)
        begin = pl.multiple_of(me * entries + chunk * width, TILE)
        pltpu.make_async_copy(
            sample.at[:, pl.ds(begin, width)], arrived.at[chunk, me], in_own.at[chunk]
        ).start()

    send_samples(0)

    feat_rows[...] = jnp.zeros_like(feat_rows)
    panel_left[...] = jnp.zeros_like(panel_left)
    right[...] = jnp.zeros_like(right)
    state4 = jnp.concatenate([state_coords[...], jnp.zeros((1, entries), F32)], axis=0)
    (s1, s2, s3), norms, ones = pieces(state4)
    state_feats[...] = jnp.concatenate([s1, s1, s2, s2, s1, s3, norms, ones], axis=0).astype(BF16)

    pltpu.make_async_copy(gathered.at[0 : regions - 1], gathered.at[0 : regions - 1], xy_recv).wait()
    pltpu.make_async_copy(
        gathered_geo.at[0 : regions - 1], gathered_geo.at[0 : regions - 1], geo_recv
    ).wait()
    ring[me, 0] = gathered[my_region]
    geo_sel[0] = gathered_geo[my_region]
    for which in range(2):
        chosen = neighbours[0, which]
        ring[me, which + 1] = gathered[chosen]
        geo_sel[which + 1] = gathered_geo[chosen]

    def around(source_z, target_z, send_sem, recv_sem):
        source = source_z * 2 + my_core
        return pltpu.make_async_remote_copy(
            src_ref=ring.at[source],
            dst_ref=ring.at[source],
            send_sem=send_sem,
            recv_sem=recv_sem,
            device_id=(my_region, target_z * 2 + my_core),
            device_id_type=MESH,
        )

    def to_sibling(source_z):
        source = source_z * 2 + my_core
        pltpu.make_async_remote_copy(
            src_ref=ring.at[source],
            dst_ref=ring.at[source],
            send_sem=sib_send,
            recv_sem=sib_recv,
            device_id=(my_region, my_z * 2 + 1 - my_core),
            device_id_type=MESH,
        ).start()

    above = (my_z + 1) % chips
    below = (my_z + chips - 1) % chips
    ups = chips // 2
    downs = chips - 1 - ups

    def up_copy(step):
        return around((my_z + chips - step) % chips, above, up_send, up_recv.at[step])

    def down_copy(step):
        return around((my_z + step) % chips, below, down_send, down_recv.at[step])

    up_copy(0).start()
    if downs > 0:
        down_copy(0).start()
    to_sibling(my_z)
    for step in range(ups):
        if step < chunks - 1:
            send_samples(step + 1)
        up_copy(step).wait_recv()
        if step + 1 < ups:
            up_copy(step + 1).start()
        to_sibling((my_z + chips - step - 1) % chips)
        if step < downs:
            down_copy(step).wait_recv()
            if step + 1 < downs:
                down_copy(step + 1).start()
            to_sibling((my_z + step + 1) % chips)
    for chunk in range(ups + 1, chunks):
        send_samples(chunk)
    pltpu.make_async_copy(ring.at[0:chips], ring.at[0:chips], sib_recv).wait()

    def prepare(which, carry):
        for source in range(devices):
            at = slice(source * rows, (source + 1) * rows)
            obs_rows[at, :] = ring[source, which, 0].astype(F32)
            innov_rows[at, :] = ring[source, which, 1].astype(F32)
        place = geo_sel[which]
        (y1, y2, y3), norms, ones = pieces(place)
        feat_rows[0:FEATS, :] = jnp.concatenate(
            [-2.0 * y1, -2.0 * y2, -2.0 * y1, -2.0 * y2, -2.0 * y3, -2.0 * y1, ones, norms], axis=0
        )
        for part in range(panels):
            lanes = slice(part * TILE, (part + 1) * TILE)
            model = obs_rows[:, lanes]
            deviation = model - jnp.sum(model, axis=0, keepdims=True) / members
            spread = (
                jnp.sum(deviation * deviation, axis=0, keepdims=True) / (members - 1)
                + place[3:4, lanes]
            )
            panel = which * panels + part
            panel_left[panel, :, 0:members] = deviation.T.astype(BF16)
            panel_left[panel, :, TILE:] = feat_rows[:, lanes].T.astype(BF16)
            panel_weight[panel] = (innov_rows[:, lanes] * (1.0 / spread)).astype(BF16)
        return carry

    lax.fori_loop(0, 3, prepare, 0)

    scale = 1.0 / (members - 1)

    def analyse_chunk(chunk, carry):
        pltpu.make_async_copy(
            arrived.at[chunk, 0 : devices - 1], arrived.at[chunk, 0 : devices - 1], in_recv.at[chunk]
        ).wait()
        pltpu.make_async_copy(arrived.at[chunk, 0], arrived.at[chunk, 0], in_own.at[chunk]).wait()
        for source in range(devices):
            fields[source * rows : (source + 1) * rows, :] = arrived[chunk, source].astype(F32)

        def analyse_block(block, carry):
            index = chunk * blocks + block
            lanes = pl.ds(pl.multiple_of(block * TILE, TILE), TILE)
            value = fields[:, lanes]
            centre = jnp.sum(value, axis=0, keepdims=True) / members
            right[0:members, 0:TILE] = (value - centre).astype(BF16)
            right[TILE : TILE + FEATS, TILE:] = state_feats[
                :, pl.ds(pl.multiple_of(index * TILE, TILE), TILE)
            ]
            total = value
            live = counts[0, index]
            for pair in range(slots // 2):
                weights = []
                for half in range(2):
                    slot = 2 * pair + half
                    panel = pattern[index, slot]
                    both = jnp.dot(panel_left[panel], right[...], preferred_element_type=F32)
                    gain = taper(both[:, TILE:], scale) * both[:, 0:TILE]
                    gains[half * TILE : (half + 1) * TILE, :] = gain.astype(BF16)
                    mask = jnp.where(slot < live, 1.0, 0.0).astype(F32)
                    weights.append(panel_weight[panel] * jnp.full((members, TILE), mask, F32).astype(BF16))
                total = total + jnp.dot(
                    jnp.concatenate(weights, axis=1), gains[...], preferred_element_type=F32
                )
            results[:, lanes] = total
            return carry

        lax.fori_loop(0, blocks, analyse_block, 0)
        for target in range(devices):
            leaving[chunk, target] = results[target * rows : (target + 1) * rows, :].astype(BF16)
        begin = pl.multiple_of(me * entries + chunk * width, TILE)

        def send_back(step, carry):
            peer = (me + step) % devices
            pltpu.make_async_remote_copy(
                src_ref=leaving.at[chunk, peer],
                dst_ref=out.at[:, pl.ds(begin, width)],
                send_sem=out_send,
                recv_sem=out_recv,
                device_id=(my_region, peer),
                device_id_type=MESH,
            ).start()
            return carry

        lax.fori_loop(1, devices, send_back, 0)
        pltpu.make_async_copy(
            leaving.at[chunk, me], out.at[:, pl.ds(begin, width)], in_own.at[chunk]
        ).start()
        return carry

    lax.fori_loop(0, chunks, analyse_chunk, 0)

    for chunk in range(chunks):
        pltpu.make_async_copy(leaving.at[chunk, 0], leaving.at[chunk, 0], in_own.at[chunk]).wait()
    others = leaving.at[:, 0 : devices - 1]
    pltpu.make_async_copy(others, others, out_recv).wait()
    pltpu.make_async_copy(others, others, out_send).wait()
    pltpu.make_async_copy(others, others, in_send).wait()
    pltpu.make_async_copy(gathered.at[0 : regions - 1], gathered.at[0 : regions - 1], xy_send).wait()
    pltpu.make_async_copy(
        gathered_geo.at[0 : regions - 1], gathered_geo.at[0 : regions - 1], geo_send
    ).wait()
    pltpu.make_async_copy(ring.at[0:ups], ring.at[0:ups], up_send).wait()
    if downs > 0:
        pltpu.make_async_copy(ring.at[0:downs], ring.at[0:downs], down_send).wait()
    pltpu.make_async_copy(ring.at[0:chips], ring.at[0:chips], sib_send).wait()


def on_device(
    regions,
    devices,
    sample_matrix,
    state_coords,
    obs_model,
    innovations,
    obs_error,
    obs_coords,
    neighbours,
    pattern,
    counts,
):
    rows = sample_matrix.shape[0]
    obs_count = obs_model.shape[1]
    entries = state_coords.shape[1]
    width = entries // CHUNKS
    members = rows * devices
    panels = 3 * obs_count // TILE
    chips = devices // 2
    vmem = pl.BlockSpec(memory_space=pltpu.VMEM)
    smem = pl.BlockSpec(memory_space=pltpu.SMEM)
    anywhere = pl.BlockSpec(memory_space=pl.ANY)
    dma = pltpu.SemaphoreType.DMA
    return pl.pallas_call(
        functools.partial(kernel, (regions, devices)),
        out_shape=jax.ShapeDtypeStruct(sample_matrix.shape, sample_matrix.dtype),
        in_specs=[anywhere, vmem, vmem, vmem, vmem, vmem, smem, smem, smem],
        out_specs=anywhere,
        scratch_shapes=[
            pltpu.VMEM((2, rows, obs_count), BF16),
            pltpu.VMEM((4, obs_count), F32),
            pltpu.VMEM((regions, 2, rows, obs_count), BF16),
            pltpu.VMEM((regions, 4, obs_count), F32),
            pltpu.VMEM((devices, 3, 2, rows, obs_count), BF16),
            pltpu.VMEM((3, 4, obs_count), F32),
            pltpu.VMEM((CHUNKS, devices, rows, width), BF16),
            pltpu.VMEM((members, width), F32),
            pltpu.VMEM((members, width), F32),
            pltpu.VMEM((CHUNKS, devices, rows, width), BF16),
            pltpu.VMEM((members, obs_count), F32),
            pltpu.VMEM((members, obs_count), F32),
            pltpu.VMEM((TILE, obs_count), F32),
            pltpu.VMEM((FEATS, entries), BF16),
            pltpu.VMEM((panels, TILE, 2 * TILE), BF16),
            pltpu.VMEM((panels, members, TILE), BF16),
            pltpu.VMEM((2 * TILE, 2 * TILE), BF16),
            pltpu.VMEM((2 * TILE, TILE), BF16),
            dma,
            dma,
            dma,
            dma,
            dma,
            dma((chips,)),
            dma,
            dma((chips,)),
            dma,
            dma,
            dma,
            dma((CHUNKS,)),
            dma((CHUNKS,)),
            dma,
            dma,
        ],
        compiler_params=pltpu.CompilerParams(
            collective_id=0, has_side_effects=True, vmem_limit_bytes=48 * 2**20
        ),
    )(
        sample_matrix,
        obs_model,
        innovations,
        obs_error.reshape(1, -1),
        obs_coords,
        state_coords,
        neighbours,
        pattern,
        counts.reshape(1, -1),
    )


def solution(mesh):
    in_specs = (
        P("member", "region"),
        P(None, ("region", "member")),
        P("member", "region"),
        P("member", "region"),
        P("region"),
        P(None, "region"),
        P("region", None),
        P(("region", "member"), None),
        P(("region", "member")),
    )
    return jax.shard_map(
        functools.partial(on_device, mesh.shape["region"], mesh.shape["member"]),
        mesh=mesh,
        in_specs=in_specs,
        out_specs=P("member", "region"),
        check_vma=False,
    )
```

```python
import functools

import jax
import jax.numpy as jnp
from jax import lax
from jax.experimental import pallas as pl
from jax.experimental.pallas import tpu as pltpu
from jax.sharding import PartitionSpec as P

MESH = pl.DeviceIdType.MESH
F32 = jnp.float32
BF16 = jnp.bfloat16
TILE = 128
FEATS = 32
HALF_WIDTH = 0.6
CHUNKS = 8
AHEAD = 2
EARLY = 2
STRIDE = 2


def wrap(index, size):
    return jnp.where(index >= size, index - size, index)


def split3(v):
    first = v.astype(BF16).astype(F32)
    rest = v - first
    second = rest.astype(BF16).astype(F32)
    third = (rest - second).astype(BF16).astype(F32)
    return first, second, third


def pieces(coords):
    row = lax.broadcasted_iota(jnp.int32, coords.shape, 0)
    scaled = jnp.where(row < 3, (coords - 0.5) * (1.0 / HALF_WIDTH), 0.0)
    norm = jnp.sum(scaled * scaled, axis=0, keepdims=True)
    n1, n2, n3 = split3(norm)
    norms = jnp.where(row == 0, n1, jnp.where(row == 1, n2, jnp.where(row == 2, n3, 0.0)))
    ones = jnp.where(row < 3, 1.0, 0.0)
    return split3(scaled), norms, ones


def taper(square, scale):
    square = jnp.maximum(square, 1e-12)
    inverse = lax.rsqrt(square)
    z = square * inverse
    near = (
        ((-0.25 * scale * z + 0.5 * scale) * z + 0.625 * scale) * z - 5.0 / 3.0 * scale
    ) * square + scale
    edge = jnp.maximum(2.0 - z, 0.0)
    edge = edge * edge
    far = (edge * edge) * ((scale / 12.0) * z + (scale / 6.0) - (scale / 24.0) * inverse)
    return jnp.where(square <= 1.0, near, far)


def kernel(
    dims,
    sample,
    obs_in,
    innov_in,
    error_in,
    obs_coords_in,
    state_coords_in,
    neighbours_in,
    pattern_in,
    counts_in,
    out,
    error,
    obs_coords,
    state_coords,
    neighbours,
    pattern,
    counts,
    load_sem,
    mine,
    geo,
    gathered,
    gathered_geo,
    ring,
    geo_sel,
    arrived,
    field_a,
    field_b,
    results,
    leaving,
    obs_rows,
    innov_rows,
    feat_rows,
    state_feats,
    panel_left,
    panel_weight,
    right_a,
    right_b,
    product_a,
    product_b,
    xy_send,
    xy_recv,
    geo_send,
    geo_recv,
    up_send,
    up_recv,
    down_send,
    down_recv,
    sib_send,
    sib_recv,
    in_send,
    in_recv,
    in_own,
    out_send,
    out_recv,
):
    regions, devices = dims
    chips = devices // 2
    rows = sample.shape[0]
    members = rows * devices
    chunks, _, _, width = arrived.shape
    entries = chunks * width
    blocks = width // TILE
    slots = pattern.shape[1]
    panels = obs_in.shape[1] // TILE
    my_region = lax.axis_index("region")
    me = lax.axis_index("member")
    my_z = me // 2
    my_core = me % 2

    loads = [
        pltpu.make_async_copy(source, target, load_sem.at[index])
        for index, (source, target) in enumerate(
            (
                (obs_in, mine.at[0]),
                (innov_in, mine.at[1]),
                (error_in, error),
                (obs_coords_in, obs_coords),
                (state_coords_in, state_coords),
                (neighbours_in, neighbours),
                (pattern_in, pattern),
                (counts_in, counts),
            )
        )
    ]
    for load in loads:
        load.start()
    barrier = pltpu.get_barrier_semaphore()

    def greet_region(step, carry):
        peer = wrap(my_region + step, regions)
        pl.semaphore_signal(barrier, inc=1, device_id=(peer, me), device_id_type=MESH)
        return carry

    def greet_member(step, carry):
        peer = wrap(me + step, devices)
        pl.semaphore_signal(barrier, inc=1, device_id=(my_region, peer), device_id_type=MESH)
        return carry

    lax.fori_loop(1, regions, greet_region, 0)
    lax.fori_loop(1, devices, greet_member, 0)
    for load in loads:
        load.wait()
    geo[0:3, :] = obs_coords[...]
    geo[3:4, :] = error[...]
    pl.semaphore_wait(barrier, regions + devices - 2)

    def send_obs(step, carry):
        pltpu.make_async_remote_copy(
            src_ref=mine,
            dst_ref=gathered.at[my_region],
            send_sem=xy_send,
            recv_sem=xy_recv,
            device_id=(wrap(my_region + step, regions), me),
            device_id_type=MESH,
        ).start()
        return carry

    def send_geo(step, carry):
        pltpu.make_async_remote_copy(
            src_ref=geo,
            dst_ref=gathered_geo.at[my_region],
            send_sem=geo_send,
            recv_sem=geo_recv,
            device_id=(wrap(my_region + step, regions), me),
            device_id_type=MESH,
        ).start()
        return carry

    def send_samples(chunk):
        def send(step, carry):
            peer = wrap(me + step, devices)
            begin = pl.multiple_of(peer * entries + chunk * width, TILE)
            pltpu.make_async_remote_copy(
                src_ref=sample.at[:, pl.ds(begin, width)],
                dst_ref=arrived.at[chunk, me],
                send_sem=in_send,
                recv_sem=in_recv.at[chunk],
                device_id=(my_region, peer),
                device_id_type=MESH,
            ).start()
            return carry

        lax.fori_loop(1, devices, send, 0)
        begin = pl.multiple_of(me * entries + chunk * width, TILE)
        pltpu.make_async_copy(
            sample.at[:, pl.ds(begin, width)], arrived.at[chunk, me], in_own.at[chunk]
        ).start()

    def around(piece, source_z, target_z, send_sem, recv_sem):
        source = wrap(source_z, chips) * 2 + my_core
        return pltpu.make_async_remote_copy(
            src_ref=ring.at[source, piece],
            dst_ref=ring.at[source, piece],
            send_sem=send_sem,
            recv_sem=recv_sem,
            device_id=(my_region, wrap(target_z, chips) * 2 + my_core),
            device_id_type=MESH,
        )

    def to_sibling(piece, source_z):
        source = wrap(source_z, chips) * 2 + my_core
        pltpu.make_async_remote_copy(
            src_ref=ring.at[source, piece],
            dst_ref=ring.at[source, piece],
            send_sem=sib_send,
            recv_sem=sib_recv,
            device_id=(my_region, my_z * 2 + 1 - my_core),
            device_id_type=MESH,
        ).start()

    ups = chips // 2
    downs = chips - 1 - ups

    def up_copy(piece, step):
        return around(piece, my_z + chips - step, my_z + 1, up_send, up_recv.at[piece, step])

    def down_copy(piece, step):
        return around(piece, my_z + step, my_z + chips - 1, down_send, down_recv.at[piece, step])

    def launch(piece):
        up_copy(piece, 0).start()
        if downs > 0:
            down_copy(piece, 0).start()
        to_sibling(piece, my_z)

    def forward(piece, step):
        up_copy(piece, step).wait_recv()
        if step + 1 < ups:
            up_copy(piece, step + 1).start()
        to_sibling(piece, my_z + chips - step - 1)
        if step < downs:
            down_copy(piece, step).wait_recv()
            if step + 1 < downs:
                down_copy(piece, step + 1).start()
            to_sibling(piece, my_z + step + 1)

    ring[me, 0] = mine[...]
    launch(0)
    lax.fori_loop(1, regions, send_obs, 0)
    for chunk in range(min(EARLY, chunks)):
        send_samples(chunk)

    feat_rows[...] = jnp.zeros_like(feat_rows)
    panel_left[...] = jnp.zeros_like(panel_left)
    right_a[...] = jnp.zeros_like(right_a)
    right_b[...] = jnp.zeros_like(right_b)
    state4 = jnp.concatenate([state_coords[...], jnp.zeros((1, entries), F32)], axis=0)
    (s1, s2, s3), norms, ones = pieces(state4)
    state_feats[...] = jnp.concatenate([s1, s1, s2, s2, s1, s3, norms, ones], axis=0).astype(BF16)

    ahead = min(AHEAD, ups)
    for step in range(ahead):
        forward(0, step)
    pltpu.make_async_copy(gathered.at[0 : regions - 1], gathered.at[0 : regions - 1], xy_recv).wait()
    for which in range(2):
        ring[me, which + 1] = gathered[neighbours[0, which]]
        launch(which + 1)
    lax.fori_loop(1, regions, send_geo, 0)
    for step in range(ups):
        if step + ahead < ups:
            forward(0, step + ahead)
        forward(1, step)
        forward(2, step)
        if step % STRIDE == 0 and EARLY + step // STRIDE < chunks:
            send_samples(EARLY + step // STRIDE)
    for chunk in range(EARLY + (ups + STRIDE - 1) // STRIDE, chunks):
        send_samples(chunk)
    pltpu.make_async_copy(
        gathered_geo.at[0 : regions - 1], gathered_geo.at[0 : regions - 1], geo_recv
    ).wait()
    geo_sel[0] = geo[...]
    for which in range(2):
        geo_sel[which + 1] = gathered_geo[neighbours[0, which]]
    pltpu.make_async_copy(ring.at[0:chips], ring.at[0:chips], sib_recv).wait()

    def prepare(which, carry):
        for source in range(devices):
            at = slice(source * rows, (source + 1) * rows)
            obs_rows[at, :] = ring[source, which, 0].astype(F32)
            innov_rows[at, :] = ring[source, which, 1].astype(F32)
        place = geo_sel[which]
        (y1, y2, y3), norms, ones = pieces(place)
        feat_rows[0:FEATS, :] = jnp.concatenate(
            [-2.0 * y1, -2.0 * y2, -2.0 * y1, -2.0 * y2, -2.0 * y3, -2.0 * y1, ones, norms], axis=0
        )
        for part in range(panels):
            lanes = slice(part * TILE, (part + 1) * TILE)
            model = obs_rows[:, lanes]
            deviation = model - jnp.sum(model, axis=0, keepdims=True) / members
            spread = (
                jnp.sum(deviation * deviation, axis=0, keepdims=True) / (members - 1)
                + place[3:4, lanes]
            )
            panel = which * panels + part
            panel_left[panel, :, 0:members] = deviation.T.astype(BF16)
            panel_left[panel, :, TILE:] = feat_rows[:, lanes].T.astype(BF16)
            panel_weight[panel] = (innov_rows[:, lanes] * (1.0 / spread)).astype(BF16)
        return carry

    lax.fori_loop(0, 3, prepare, 0)

    scale = 1.0 / (members - 1)

    def await_chunk(chunk):
        pltpu.make_async_copy(
            arrived.at[chunk, 0 : devices - 1], arrived.at[chunk, 0 : devices - 1], in_recv.at[chunk]
        ).wait()
        pltpu.make_async_copy(arrived.at[chunk, 0], arrived.at[chunk, 0], in_own.at[chunk]).wait()

    def products(chunk, block, field, right, product):
        index = chunk * blocks + block
        lanes = slice(block * TILE, (block + 1) * TILE)
        for source in range(devices):
            field[source * rows : (source + 1) * rows, :] = arrived[chunk, source, :, lanes].astype(F32)
        value = field[...]
        centre = jnp.sum(value, axis=0, keepdims=True) / members
        right[0:members, 0:TILE] = (value - centre).astype(BF16)
        right[TILE : TILE + FEATS, TILE:] = state_feats[
            :, pl.ds(pl.multiple_of(index * TILE, TILE), TILE)
        ]
        left = jnp.concatenate([panel_left[pattern[index, slot]] for slot in range(slots)], axis=0)
        product[...] = jnp.dot(left, right[...], preferred_element_type=F32)

    def update(chunk, block, field, product):
        index = chunk * blocks + block
        live = counts[0, index]
        gains, weights = [], []
        for slot in range(slots):
            at = slice(slot * TILE, (slot + 1) * TILE)
            gains.append((taper(product[at, TILE:], scale) * product[at, 0:TILE]).astype(BF16))
            mask = jnp.where(slot < live, 1.0, 0.0).astype(F32)
            weights.append(
                panel_weight[pattern[index, slot]] * jnp.full((members, TILE), mask, F32).astype(BF16)
            )
        results[:, block * TILE : (block + 1) * TILE] = field[...] + jnp.dot(
            jnp.concatenate(weights, axis=1),
            jnp.concatenate(gains, axis=0),
            preferred_element_type=F32,
        )

    await_chunk(0)
    products(0, 0, field_a, right_a, product_a)

    def analyse_chunk(chunk, carry):
        for block in range(0, blocks, 2):
            products(chunk, block + 1, field_b, right_b, product_b)
            update(chunk, block, field_a, product_a)
            if block + 2 < blocks:
                products(chunk, block + 2, field_a, right_a, product_a)
            else:

                @pl.when(chunk + 1 < chunks)
                def _():
                    await_chunk(chunk + 1)

                coming = jnp.minimum(chunk + 1, chunks - 1)
                products(coming, 0, field_a, right_a, product_a)
            update(chunk, block + 1, field_b, product_b)
        for target in range(devices):
            leaving[chunk, target] = results[target * rows : (target + 1) * rows, :].astype(BF16)
        begin = pl.multiple_of(me * entries + chunk * width, TILE)

        def send_back(step, carry):
            peer = wrap(me + step, devices)
            pltpu.make_async_remote_copy(
                src_ref=leaving.at[chunk, peer],
                dst_ref=out.at[:, pl.ds(begin, width)],
                send_sem=out_send,
                recv_sem=out_recv,
                device_id=(my_region, peer),
                device_id_type=MESH,
            ).start()
            return carry

        lax.fori_loop(1, devices, send_back, 0)
        pltpu.make_async_copy(
            leaving.at[chunk, me], out.at[:, pl.ds(begin, width)], in_own.at[chunk]
        ).start()
        return carry

    lax.fori_loop(0, chunks, analyse_chunk, 0)

    for chunk in range(chunks):
        pltpu.make_async_copy(leaving.at[chunk, 0], leaving.at[chunk, 0], in_own.at[chunk]).wait()
    others = leaving.at[:, 0 : devices - 1]
    pltpu.make_async_copy(others, others, out_recv).wait()
    pltpu.make_async_copy(others, others, out_send).wait()
    pltpu.make_async_copy(others, others, in_send).wait()
    pltpu.make_async_copy(gathered.at[0 : regions - 1], gathered.at[0 : regions - 1], xy_send).wait()
    pltpu.make_async_copy(
        gathered_geo.at[0 : regions - 1], gathered_geo.at[0 : regions - 1], geo_send
    ).wait()
    pltpu.make_async_copy(ring.at[0:ups], ring.at[0:ups], up_send).wait()
    if downs > 0:
        pltpu.make_async_copy(ring.at[0:downs], ring.at[0:downs], down_send).wait()
    pltpu.make_async_copy(ring.at[0:chips], ring.at[0:chips], sib_send).wait()


def on_device(
    regions,
    devices,
    sample_matrix,
    state_coords,
    obs_model,
    innovations,
    obs_error,
    obs_coords,
    neighbours,
    pattern,
    counts,
):
    rows = sample_matrix.shape[0]
    obs_count = obs_model.shape[1]
    entries = state_coords.shape[1]
    width = entries // CHUNKS
    members = rows * devices
    panels = 3 * obs_count // TILE
    slots = pattern.shape[1]
    chips = devices // 2
    hbm = pl.BlockSpec(memory_space=pltpu.HBM)
    dma = pltpu.SemaphoreType.DMA
    return pl.pallas_call(
        functools.partial(kernel, (regions, devices)),
        out_shape=jax.ShapeDtypeStruct(sample_matrix.shape, sample_matrix.dtype),
        in_specs=[hbm] * 9,
        out_specs=hbm,
        scratch_shapes=[
            pltpu.VMEM((1, obs_count), F32),
            pltpu.VMEM(obs_coords.shape, F32),
            pltpu.VMEM(state_coords.shape, F32),
            pltpu.SMEM(neighbours.shape, jnp.int32),
            pltpu.SMEM(pattern.shape, jnp.int32),
            pltpu.SMEM((1, counts.shape[0]), jnp.int32),
            dma((8,)),
            pltpu.VMEM((2, rows, obs_count), BF16),
            pltpu.VMEM((4, obs_count), F32),
            pltpu.VMEM((regions, 2, rows, obs_count), BF16),
            pltpu.VMEM((regions, 4, obs_count), F32),
            pltpu.VMEM((devices, 3, 2, rows, obs_count), BF16),
            pltpu.VMEM((3, 4, obs_count), F32),
            pltpu.VMEM((CHUNKS, devices, rows, width), BF16),
            pltpu.VMEM((members, TILE), F32),
            pltpu.VMEM((members, TILE), F32),
            pltpu.VMEM((members, width), F32),
            pltpu.VMEM((CHUNKS, devices, rows, width), BF16),
            pltpu.VMEM((members, obs_count), F32),
            pltpu.VMEM((members, obs_count), F32),
            pltpu.VMEM((TILE, obs_count), F32),
            pltpu.VMEM((FEATS, entries), BF16),
            pltpu.VMEM((panels, TILE, 2 * TILE), BF16),
            pltpu.VMEM((panels, members, TILE), BF16),
            pltpu.VMEM((2 * TILE, 2 * TILE), BF16),
            pltpu.VMEM((2 * TILE, 2 * TILE), BF16),
            pltpu.VMEM((slots * TILE, 2 * TILE), F32),
            pltpu.VMEM((slots * TILE, 2 * TILE), F32),
            dma,
            dma,
            dma,
            dma,
            dma,
            dma((3, chips)),
            dma,
            dma((3, chips)),
            dma,
            dma,
            dma,
            dma((CHUNKS,)),
            dma((CHUNKS,)),
            dma,
            dma,
        ],
        compiler_params=pltpu.CompilerParams(
            collective_id=0, has_side_effects=True, vmem_limit_bytes=60 * 2**20
        ),
    )(
        sample_matrix,
        obs_model,
        innovations,
        obs_error.reshape(1, -1),
        obs_coords,
        state_coords,
        neighbours,
        pattern,
        counts.reshape(1, -1),
    )


def solution(mesh):
    in_specs = (
        P("member", "region"),
        P(None, ("region", "member")),
        P("member", "region"),
        P("member", "region"),
        P("region"),
        P(None, "region"),
        P("region", None),
        P(("region", "member"), None),
        P(("region", "member")),
    )
    return jax.shard_map(
        functools.partial(on_device, mesh.shape["region"], mesh.shape["member"]),
        mesh=mesh,
        in_specs=in_specs,
        out_specs=P("member", "region"),
        check_vma=False,
    )
```

```python
import functools

import jax
import jax.numpy as jnp
from jax import lax
from jax.experimental import pallas as pl
from jax.experimental.pallas import tpu as pltpu
from jax.sharding import PartitionSpec as P

MESH = pl.DeviceIdType.MESH
F32 = jnp.float32
BF16 = jnp.bfloat16
TILE = 128
FEATS = 32
HALF_WIDTH = 0.6
CHUNKS = 8
SPREAD = (((0, 3), (0, 1)), ((3, 6), (3, 4), (1, 2)), ((6, 8), (6, 7), (4, 5)))
SENT = (2, 1, 1, 1)


def wrap(index, size):
    return jnp.where(index >= size, index - size, index)


def split3(v):
    first = v.astype(BF16).astype(F32)
    rest = v - first
    second = rest.astype(BF16).astype(F32)
    third = (rest - second).astype(BF16).astype(F32)
    return first, second, third


def pieces(coords):
    row = lax.broadcasted_iota(jnp.int32, coords.shape, 0)
    scaled = jnp.where(row < 3, (coords - 0.5) * (1.0 / HALF_WIDTH), 0.0)
    norm = jnp.sum(scaled * scaled, axis=0, keepdims=True)
    n1, n2, n3 = split3(norm)
    norms = jnp.where(row == 0, n1, jnp.where(row == 1, n2, jnp.where(row == 2, n3, 0.0)))
    ones = jnp.where(row < 3, 1.0, 0.0)
    return split3(scaled), norms, ones


def taper(square, scale):
    square = jnp.maximum(square, 1e-12)
    inverse = lax.rsqrt(square)
    z = square * inverse
    near = (
        ((-0.25 * scale * z + 0.5 * scale) * z + 0.625 * scale) * z - 5.0 / 3.0 * scale
    ) * square + scale
    edge = jnp.maximum(2.0 - z, 0.0)
    edge = edge * edge
    far = (edge * edge) * ((scale / 12.0) * z + (scale / 6.0) - (scale / 24.0) * inverse)
    return jnp.where(square <= 1.0, near, far)


def kernel(
    dims,
    sample,
    obs_in,
    innov_in,
    error_in,
    obs_coords_in,
    state_coords_in,
    neighbours_in,
    pattern_in,
    counts_in,
    out,
    error,
    obs_coords,
    state_coords,
    neighbours,
    pattern,
    counts,
    load_sem,
    mine,
    geo,
    gathered,
    gathered_geo,
    ring,
    geo_sel,
    arrived,
    field_a,
    field_b,
    results,
    leaving,
    obs_rows,
    innov_rows,
    feat_rows,
    state_feats,
    panel_left,
    panel_weight,
    right_a,
    right_b,
    product_a,
    product_b,
    xy_send,
    xy_recv,
    geo_send,
    geo_recv,
    up_send,
    up_recv,
    down_send,
    down_recv,
    sib_send,
    sib_recv,
    in_send,
    in_recv,
    in_own,
    out_send,
    out_recv,
):
    regions, devices = dims
    chips = devices // 2
    rows = sample.shape[0]
    members = rows * devices
    chunks, _, _, width = arrived.shape
    entries = chunks * width
    blocks = width // TILE
    slots = pattern.shape[1]
    panels = obs_in.shape[1] // TILE
    my_region = lax.axis_index("region")
    me = lax.axis_index("member")
    my_z = me // 2
    my_core = me % 2

    loads = [
        pltpu.make_async_copy(source, target, load_sem.at[index])
        for index, (source, target) in enumerate(
            (
                (obs_in, mine.at[0]),
                (innov_in, mine.at[1]),
                (error_in, error),
                (obs_coords_in, obs_coords),
                (state_coords_in, state_coords),
                (neighbours_in, neighbours),
                (pattern_in, pattern),
                (counts_in, counts),
            )
        )
    ]
    for load in loads:
        load.start()
    barrier = pltpu.get_barrier_semaphore()

    def greet_region(step, carry):
        peer = wrap(my_region + step, regions)
        pl.semaphore_signal(barrier, inc=1, device_id=(peer, me), device_id_type=MESH)
        return carry

    def greet_member(step, carry):
        peer = wrap(me + step, devices)
        pl.semaphore_signal(barrier, inc=1, device_id=(my_region, peer), device_id_type=MESH)
        return carry

    lax.fori_loop(1, regions, greet_region, 0)
    lax.fori_loop(1, devices, greet_member, 0)
    for load in loads:
        load.wait()
    geo[0:3, :] = obs_coords[...]
    geo[3:4, :] = error[...]
    pl.semaphore_wait(barrier, regions + devices - 2)

    def send_obs(step, carry):
        pltpu.make_async_remote_copy(
            src_ref=mine,
            dst_ref=gathered.at[my_region],
            send_sem=xy_send,
            recv_sem=xy_recv,
            device_id=(wrap(my_region + step, regions), me),
            device_id_type=MESH,
        ).start()
        return carry

    def send_geo(step, carry):
        pltpu.make_async_remote_copy(
            src_ref=geo,
            dst_ref=gathered_geo.at[my_region],
            send_sem=geo_send,
            recv_sem=geo_recv,
            device_id=(wrap(my_region + step, regions), me),
            device_id_type=MESH,
        ).start()
        return carry

    def send_samples(chunk):
        def send(step, carry):
            peer = wrap(me + step, devices)
            begin = pl.multiple_of(peer * entries + chunk * width, TILE)
            pltpu.make_async_remote_copy(
                src_ref=sample.at[:, pl.ds(begin, width)],
                dst_ref=arrived.at[chunk, me],
                send_sem=in_send,
                recv_sem=in_recv.at[chunk],
                device_id=(my_region, peer),
                device_id_type=MESH,
            ).start()
            return carry

        lax.fori_loop(1, devices, send, 0)
        begin = pl.multiple_of(me * entries + chunk * width, TILE)
        pltpu.make_async_copy(
            sample.at[:, pl.ds(begin, width)], arrived.at[chunk, me], in_own.at[chunk]
        ).start()

    span = (slice(0, 1), slice(1, 3))
    ups = chips // 2
    downs = chips - 1 - ups

    def hop(piece, source_z, target_z, send_sem, recv_sem):
        source = wrap(source_z, chips) * 2 + my_core
        return pltpu.make_async_remote_copy(
            src_ref=ring.at[source, span[piece]],
            dst_ref=ring.at[source, span[piece]],
            send_sem=send_sem,
            recv_sem=recv_sem,
            device_id=(my_region, wrap(target_z, chips) * 2 + my_core),
            device_id_type=MESH,
        )

    def up_copy(piece, done, goal):
        return hop(
            piece, my_z + chips - done, my_z + goal - done, up_send, up_recv.at[piece, goal - 1]
        )

    def down_copy(piece, done, goal):
        return hop(
            piece, my_z + done, my_z + chips - goal + done, down_send, down_recv.at[piece, goal - 1]
        )

    def to_sibling(piece, source_z):
        source = wrap(source_z, chips) * 2 + my_core
        pltpu.make_async_remote_copy(
            src_ref=ring.at[source, span[piece]],
            dst_ref=ring.at[source, span[piece]],
            send_sem=sib_send,
            recv_sem=sib_recv,
            device_id=(my_region, my_z * 2 + 1 - my_core),
            device_id_type=MESH,
        ).start()

    def pass_on(piece, copy, reach, at):
        for edges in SPREAD:
            for done, goal in edges:
                if done == at and goal <= reach:
                    copy(piece, done, goal).start()

    def launch(piece):
        pass_on(piece, up_copy, ups, 0)
        pass_on(piece, down_copy, downs, 0)
        to_sibling(piece, my_z)

    def forward(piece, round_at):
        for done, goal in SPREAD[round_at]:
            if goal <= ups:
                up_copy(piece, done, goal).wait_recv()
                pass_on(piece, up_copy, ups, goal)
                to_sibling(piece, my_z + chips - goal)
            if goal <= downs:
                down_copy(piece, done, goal).wait_recv()
                pass_on(piece, down_copy, downs, goal)
                to_sibling(piece, my_z + goal)

    ring[me, 0] = mine[...]
    launch(0)
    lax.fori_loop(1, regions, send_obs, 0)
    bounds = [min(sum(SENT[:count]), chunks) for count in range(len(SENT) + 1)] + [chunks]

    def send_part(part):
        for chunk in range(bounds[part], bounds[part + 1]):
            send_samples(chunk)

    send_part(0)

    feat_rows[...] = jnp.zeros_like(feat_rows)
    panel_left[...] = jnp.zeros_like(panel_left)
    right_a[...] = jnp.zeros_like(right_a)
    right_b[...] = jnp.zeros_like(right_b)
    state4 = jnp.concatenate([state_coords[...], jnp.zeros((1, entries), F32)], axis=0)
    (s1, s2, s3), norms, ones = pieces(state4)
    state_feats[...] = jnp.concatenate([s1, s1, s2, s2, s1, s3, norms, ones], axis=0).astype(BF16)

    forward(0, 0)
    pltpu.make_async_copy(gathered.at[0 : regions - 1], gathered.at[0 : regions - 1], xy_recv).wait()
    for which in range(2):
        ring[me, which + 1] = gathered[neighbours[0, which]]
    launch(1)
    lax.fori_loop(1, regions, send_geo, 0)
    send_part(1)
    forward(0, 1)
    forward(1, 0)
    send_part(2)
    forward(0, 2)
    forward(1, 1)
    send_part(3)
    forward(1, 2)
    send_part(4)
    pltpu.make_async_copy(
        gathered_geo.at[0 : regions - 1], gathered_geo.at[0 : regions - 1], geo_recv
    ).wait()
    geo_sel[0] = geo[...]
    for which in range(2):
        geo_sel[which + 1] = gathered_geo[neighbours[0, which]]
    pltpu.make_async_copy(ring.at[0:chips], ring.at[0:chips], sib_recv).wait()

    def prepare(which, carry):
        for source in range(devices):
            at = slice(source * rows, (source + 1) * rows)
            obs_rows[at, :] = ring[source, which, 0].astype(F32)
            innov_rows[at, :] = ring[source, which, 1].astype(F32)
        place = geo_sel[which]
        (y1, y2, y3), norms, ones = pieces(place)
        feat_rows[0:FEATS, :] = jnp.concatenate(
            [-2.0 * y1, -2.0 * y2, -2.0 * y1, -2.0 * y2, -2.0 * y3, -2.0 * y1, ones, norms], axis=0
        )
        for part in range(panels):
            lanes = slice(part * TILE, (part + 1) * TILE)
            model = obs_rows[:, lanes]
            deviation = model - jnp.sum(model, axis=0, keepdims=True) / members
            spread = (
                jnp.sum(deviation * deviation, axis=0, keepdims=True) / (members - 1)
                + place[3:4, lanes]
            )
            panel = which * panels + part
            panel_left[panel, :, 0:members] = deviation.T.astype(BF16)
            panel_left[panel, :, TILE:] = feat_rows[:, lanes].T.astype(BF16)
            panel_weight[panel] = (innov_rows[:, lanes] * (1.0 / spread)).astype(BF16)
        return carry

    lax.fori_loop(0, 3, prepare, 0)

    scale = 1.0 / (members - 1)

    def await_chunk(chunk):
        pltpu.make_async_copy(
            arrived.at[chunk, 0 : devices - 1], arrived.at[chunk, 0 : devices - 1], in_recv.at[chunk]
        ).wait()
        pltpu.make_async_copy(arrived.at[chunk, 0], arrived.at[chunk, 0], in_own.at[chunk]).wait()

    def products(chunk, block, field, right, product):
        index = chunk * blocks + block
        lanes = slice(block * TILE, (block + 1) * TILE)
        for source in range(devices):
            field[source * rows : (source + 1) * rows, :] = arrived[chunk, source, :, lanes].astype(F32)
        value = field[...]
        centre = jnp.sum(value, axis=0, keepdims=True) / members
        right[0:members, 0:TILE] = (value - centre).astype(BF16)
        right[TILE : TILE + FEATS, TILE:] = state_feats[
            :, pl.ds(pl.multiple_of(index * TILE, TILE), TILE)
        ]
        left = jnp.concatenate([panel_left[pattern[index, slot]] for slot in range(slots)], axis=0)
        product[...] = jnp.dot(left, right[...], preferred_element_type=F32)

    def update(chunk, block, field, product):
        index = chunk * blocks + block
        live = counts[0, index]
        gains, weights = [], []
        for slot in range(slots):
            at = slice(slot * TILE, (slot + 1) * TILE)
            gains.append((taper(product[at, TILE:], scale) * product[at, 0:TILE]).astype(BF16))
            mask = jnp.where(slot < live, 1.0, 0.0).astype(F32)
            weights.append(
                panel_weight[pattern[index, slot]] * jnp.full((members, TILE), mask, F32).astype(BF16)
            )
        results[:, block * TILE : (block + 1) * TILE] = field[...] + jnp.dot(
            jnp.concatenate(weights, axis=1),
            jnp.concatenate(gains, axis=0),
            preferred_element_type=F32,
        )

    await_chunk(0)
    products(0, 0, field_a, right_a, product_a)

    def analyse_chunk(chunk, carry):
        for block in range(0, blocks, 2):
            products(chunk, block + 1, field_b, right_b, product_b)
            update(chunk, block, field_a, product_a)
            if block + 2 < blocks:
                products(chunk, block + 2, field_a, right_a, product_a)
            else:

                @pl.when(chunk + 1 < chunks)
                def _():
                    await_chunk(chunk + 1)

                coming = jnp.minimum(chunk + 1, chunks - 1)
                products(coming, 0, field_a, right_a, product_a)
            update(chunk, block + 1, field_b, product_b)
        for target in range(devices):
            leaving[chunk, target] = results[target * rows : (target + 1) * rows, :].astype(BF16)
        begin = pl.multiple_of(me * entries + chunk * width, TILE)

        def send_back(step, carry):
            peer = wrap(me + step, devices)
            pltpu.make_async_remote_copy(
                src_ref=leaving.at[chunk, peer],
                dst_ref=out.at[:, pl.ds(begin, width)],
                send_sem=out_send,
                recv_sem=out_recv,
                device_id=(my_region, peer),
                device_id_type=MESH,
            ).start()
            return carry

        lax.fori_loop(1, devices, send_back, 0)
        pltpu.make_async_copy(
            leaving.at[chunk, me], out.at[:, pl.ds(begin, width)], in_own.at[chunk]
        ).start()
        return carry

    lax.fori_loop(0, chunks, analyse_chunk, 0)

    for chunk in range(chunks):
        pltpu.make_async_copy(leaving.at[chunk, 0], leaving.at[chunk, 0], in_own.at[chunk]).wait()
    others = leaving.at[:, 0 : devices - 1]
    pltpu.make_async_copy(others, others, out_recv).wait()
    pltpu.make_async_copy(others, others, out_send).wait()
    pltpu.make_async_copy(others, others, in_send).wait()
    pltpu.make_async_copy(gathered.at[0 : regions - 1], gathered.at[0 : regions - 1], xy_send).wait()
    pltpu.make_async_copy(
        gathered_geo.at[0 : regions - 1], gathered_geo.at[0 : regions - 1], geo_send
    ).wait()
    pltpu.make_async_copy(ring.at[0:ups], ring.at[0:ups], up_send).wait()
    if downs > 0:
        pltpu.make_async_copy(ring.at[0:downs], ring.at[0:downs], down_send).wait()
    pltpu.make_async_copy(ring.at[0:chips], ring.at[0:chips], sib_send).wait()


def on_device(
    regions,
    devices,
    sample_matrix,
    state_coords,
    obs_model,
    innovations,
    obs_error,
    obs_coords,
    neighbours,
    pattern,
    counts,
):
    rows = sample_matrix.shape[0]
    obs_count = obs_model.shape[1]
    entries = state_coords.shape[1]
    width = entries // CHUNKS
    members = rows * devices
    panels = 3 * obs_count // TILE
    slots = pattern.shape[1]
    chips = devices // 2
    hbm = pl.BlockSpec(memory_space=pltpu.HBM)
    dma = pltpu.SemaphoreType.DMA
    return pl.pallas_call(
        functools.partial(kernel, (regions, devices)),
        out_shape=jax.ShapeDtypeStruct(sample_matrix.shape, sample_matrix.dtype),
        in_specs=[hbm] * 9,
        out_specs=hbm,
        scratch_shapes=[
            pltpu.VMEM((1, obs_count), F32),
            pltpu.VMEM(obs_coords.shape, F32),
            pltpu.VMEM(state_coords.shape, F32),
            pltpu.SMEM(neighbours.shape, jnp.int32),
            pltpu.SMEM(pattern.shape, jnp.int32),
            pltpu.SMEM((1, counts.shape[0]), jnp.int32),
            dma((8,)),
            pltpu.VMEM((2, rows, obs_count), BF16),
            pltpu.VMEM((4, obs_count), F32),
            pltpu.VMEM((regions, 2, rows, obs_count), BF16),
            pltpu.VMEM((regions, 4, obs_count), F32),
            pltpu.VMEM((devices, 3, 2, rows, obs_count), BF16),
            pltpu.VMEM((3, 4, obs_count), F32),
            pltpu.VMEM((CHUNKS, devices, rows, width), BF16),
            pltpu.VMEM((members, TILE), F32),
            pltpu.VMEM((members, TILE), F32),
            pltpu.VMEM((members, width), F32),
            pltpu.VMEM((CHUNKS, devices, rows, width), BF16),
            pltpu.VMEM((members, obs_count), F32),
            pltpu.VMEM((members, obs_count), F32),
            pltpu.VMEM((TILE, obs_count), F32),
            pltpu.VMEM((FEATS, entries), BF16),
            pltpu.VMEM((panels, TILE, 2 * TILE), BF16),
            pltpu.VMEM((panels, members, TILE), BF16),
            pltpu.VMEM((2 * TILE, 2 * TILE), BF16),
            pltpu.VMEM((2 * TILE, 2 * TILE), BF16),
            pltpu.VMEM((slots * TILE, 2 * TILE), F32),
            pltpu.VMEM((slots * TILE, 2 * TILE), F32),
            dma,
            dma,
            dma,
            dma,
            dma,
            dma((2, chips)),
            dma,
            dma((2, chips)),
            dma,
            dma,
            dma,
            dma((CHUNKS,)),
            dma((CHUNKS,)),
            dma,
            dma,
        ],
        compiler_params=pltpu.CompilerParams(
            collective_id=0, has_side_effects=True, vmem_limit_bytes=60 * 2**20
        ),
    )(
        sample_matrix,
        obs_model,
        innovations,
        obs_error.reshape(1, -1),
        obs_coords,
        state_coords,
        neighbours,
        pattern,
        counts.reshape(1, -1),
    )


def solution(mesh):
    in_specs = (
        P("member", "region"),
        P(None, ("region", "member")),
        P("member", "region"),
        P("member", "region"),
        P("region"),
        P(None, "region"),
        P("region", None),
        P(("region", "member"), None),
        P(("region", "member")),
    )
    return jax.shard_map(
        functools.partial(on_device, mesh.shape["region"], mesh.shape["member"]),
        mesh=mesh,
        in_specs=in_specs,
        out_specs=P("member", "region"),
        check_vma=False,
    )
```

```python
import functools

import jax
import jax.numpy as jnp
from jax import lax
from jax.experimental import pallas as pl
from jax.experimental.pallas import tpu as pltpu
from jax.sharding import PartitionSpec as P

MESH = pl.DeviceIdType.MESH
F32 = jnp.float32
BF16 = jnp.bfloat16
TILE = 128
FEATS = 32
HALF_WIDTH = 0.6
CHUNKS = 8
SPREAD = (((0, 3), (0, 1)), ((3, 6), (3, 4), (1, 2)), ((6, 8), (6, 7), (4, 5)))
SENT = (2, 1, 1, 1)


def wrap(index, size):
    return jnp.where(index >= size, index - size, index)


def split3(v):
    first = v.astype(BF16).astype(F32)
    rest = v - first
    second = rest.astype(BF16).astype(F32)
    third = (rest - second).astype(BF16).astype(F32)
    return first, second, third


def pieces(coords):
    row = lax.broadcasted_iota(jnp.int32, coords.shape, 0)
    scaled = jnp.where(row < 3, (coords - 0.5) * (1.0 / HALF_WIDTH), 0.0)
    norm = jnp.sum(scaled * scaled, axis=0, keepdims=True)
    n1, n2, n3 = split3(norm)
    norms = jnp.where(row == 0, n1, jnp.where(row == 1, n2, jnp.where(row == 2, n3, 0.0)))
    ones = jnp.where(row < 3, 1.0, 0.0)
    return split3(scaled), norms, ones


def taper(square, scale):
    square = jnp.maximum(square, 1e-12)
    inverse = lax.rsqrt(square)
    z = square * inverse
    near = (
        ((-0.25 * scale * z + 0.5 * scale) * z + 0.625 * scale) * z - 5.0 / 3.0 * scale
    ) * square + scale
    edge = jnp.maximum(2.0 - z, 0.0)
    edge = edge * edge
    far = (edge * edge) * ((scale / 12.0) * z + (scale / 6.0) - (scale / 24.0) * inverse)
    return jnp.where(square <= 1.0, near, far)


def kernel(
    dims,
    sample,
    obs_in,
    innov_in,
    error_in,
    obs_coords_in,
    state_coords_in,
    neighbours_in,
    pattern_in,
    counts_in,
    out,
    error,
    obs_coords,
    state_coords,
    neighbours,
    pattern,
    counts,
    load_sem,
    mine,
    geo,
    gathered,
    gathered_geo,
    ring,
    geo_sel,
    arrived,
    field_a,
    field_b,
    results,
    leaving,
    obs_rows,
    innov_rows,
    feat_rows,
    state_feats,
    panel_left,
    panel_weight,
    right_a,
    right_b,
    product_a,
    product_b,
    xy_send,
    xy_recv,
    geo_send,
    geo_recv,
    up_send,
    up_recv,
    down_send,
    down_recv,
    sib_send,
    sib_recv,
    in_send,
    in_recv,
    in_own,
    out_send,
    out_recv,
):
    regions, devices = dims
    chips = devices // 2
    rows = sample.shape[0]
    members = rows * devices
    chunks, _, _, width = arrived.shape
    entries = chunks * width
    blocks = width // TILE
    slots = pattern.shape[1]
    panels = obs_in.shape[1] // TILE
    my_region = lax.axis_index("region")
    me = lax.axis_index("member")
    my_z = me // 2
    my_core = me % 2

    loads = [
        pltpu.make_async_copy(source, target, load_sem.at[index])
        for index, (source, target) in enumerate(
            (
                (obs_in, mine.at[0]),
                (innov_in, mine.at[1]),
                (error_in, error),
                (obs_coords_in, obs_coords),
                (state_coords_in, state_coords),
                (neighbours_in, neighbours),
                (pattern_in, pattern),
                (counts_in, counts),
            )
        )
    ]
    for load in loads:
        load.start()
    barrier = pltpu.get_barrier_semaphore()

    def greet_region(step, carry):
        peer = wrap(my_region + step, regions)
        pl.semaphore_signal(barrier, inc=1, device_id=(peer, me), device_id_type=MESH)
        return carry

    def greet_member(step, carry):
        peer = wrap(me + step, devices)
        pl.semaphore_signal(barrier, inc=1, device_id=(my_region, peer), device_id_type=MESH)
        return carry

    lax.fori_loop(1, regions, greet_region, 0)
    lax.fori_loop(1, devices, greet_member, 0)
    for load in loads:
        load.wait()
    geo[0:3, :] = obs_coords[...]
    geo[3:4, :] = error[...]
    pl.semaphore_wait(barrier, regions + devices - 2)

    def send_obs(step, carry):
        pltpu.make_async_remote_copy(
            src_ref=mine,
            dst_ref=gathered.at[my_region],
            send_sem=xy_send,
            recv_sem=xy_recv,
            device_id=(wrap(my_region + step, regions), me),
            device_id_type=MESH,
        ).start()
        return carry

    def send_geo(step, carry):
        pltpu.make_async_remote_copy(
            src_ref=geo,
            dst_ref=gathered_geo.at[my_region],
            send_sem=geo_send,
            recv_sem=geo_recv,
            device_id=(wrap(my_region + step, regions), me),
            device_id_type=MESH,
        ).start()
        return carry

    def send_samples(chunk):
        def send(step, carry):
            peer = wrap(me + step, devices)
            begin = pl.multiple_of(peer * entries + chunk * width, TILE)
            pltpu.make_async_remote_copy(
                src_ref=sample.at[:, pl.ds(begin, width)],
                dst_ref=arrived.at[chunk, me],
                send_sem=in_send,
                recv_sem=in_recv.at[chunk],
                device_id=(my_region, peer),
                device_id_type=MESH,
            ).start()
            return carry

        lax.fori_loop(1, devices, send, 0)
        begin = pl.multiple_of(me * entries + chunk * width, TILE)
        pltpu.make_async_copy(
            sample.at[:, pl.ds(begin, width)], arrived.at[chunk, me], in_own.at[chunk]
        ).start()

    span = (slice(0, 1), slice(1, 3))
    ups = (chips - 1) // 2
    downs = chips - 1 - ups

    def hop(piece, source_z, target_z, send_sem, recv_sem):
        source = wrap(source_z, chips) * 2 + my_core
        return pltpu.make_async_remote_copy(
            src_ref=ring.at[source, span[piece]],
            dst_ref=ring.at[source, span[piece]],
            send_sem=send_sem,
            recv_sem=recv_sem,
            device_id=(my_region, wrap(target_z, chips) * 2 + my_core),
            device_id_type=MESH,
        )

    def up_copy(piece, done, goal):
        return hop(
            piece, my_z + chips - done, my_z + goal - done, up_send, up_recv.at[piece, goal - 1]
        )

    def down_copy(piece, done, goal):
        return hop(
            piece, my_z + done, my_z + chips - goal + done, down_send, down_recv.at[piece, goal - 1]
        )

    def to_sibling(piece, source_z):
        source = wrap(source_z, chips) * 2 + my_core
        pltpu.make_async_remote_copy(
            src_ref=ring.at[source, span[piece]],
            dst_ref=ring.at[source, span[piece]],
            send_sem=sib_send,
            recv_sem=sib_recv,
            device_id=(my_region, my_z * 2 + 1 - my_core),
            device_id_type=MESH,
        ).start()

    def pass_on(piece, copy, reach, at):
        for edges in SPREAD:
            for done, goal in edges:
                if done == at and goal <= reach:
                    copy(piece, done, goal).start()

    def launch(piece):
        pass_on(piece, up_copy, ups, 0)
        pass_on(piece, down_copy, downs, 0)
        to_sibling(piece, my_z)

    def forward(piece, round_at):
        for done, goal in SPREAD[round_at]:
            if goal <= ups:
                up_copy(piece, done, goal).wait_recv()
                pass_on(piece, up_copy, ups, goal)
                to_sibling(piece, my_z + chips - goal)
            if goal <= downs:
                down_copy(piece, done, goal).wait_recv()
                pass_on(piece, down_copy, downs, goal)
                to_sibling(piece, my_z + goal)

    ring[me, 0] = mine[...]
    launch(0)
    lax.fori_loop(1, regions, send_obs, 0)
    bounds = [min(sum(SENT[:count]), chunks) for count in range(len(SENT) + 1)] + [chunks]

    def send_part(part):
        for chunk in range(bounds[part], bounds[part + 1]):
            send_samples(chunk)

    send_part(0)

    feat_rows[...] = jnp.zeros_like(feat_rows)
    panel_left[...] = jnp.zeros_like(panel_left)
    right_a[...] = jnp.zeros_like(right_a)
    right_b[...] = jnp.zeros_like(right_b)
    state4 = jnp.concatenate([state_coords[...], jnp.zeros((1, entries), F32)], axis=0)
    (s1, s2, s3), norms, ones = pieces(state4)
    state_feats[...] = jnp.concatenate([s1, s1, s2, s2, s1, s3, norms, ones], axis=0).astype(BF16)

    forward(0, 0)
    pltpu.make_async_copy(gathered.at[0 : regions - 1], gathered.at[0 : regions - 1], xy_recv).wait()
    for which in range(2):
        ring[me, which + 1] = gathered[neighbours[0, which]]
    launch(1)
    lax.fori_loop(1, regions, send_geo, 0)
    send_part(1)
    forward(0, 1)
    forward(1, 0)
    send_part(2)
    forward(0, 2)
    forward(1, 1)
    send_part(3)
    forward(1, 2)
    send_part(4)
    pltpu.make_async_copy(
        gathered_geo.at[0 : regions - 1], gathered_geo.at[0 : regions - 1], geo_recv
    ).wait()
    geo_sel[0] = geo[...]
    for which in range(2):
        geo_sel[which + 1] = gathered_geo[neighbours[0, which]]
    pltpu.make_async_copy(ring.at[0:chips], ring.at[0:chips], sib_recv).wait()

    def prepare(which, carry):
        for source in range(devices):
            at = slice(source * rows, (source + 1) * rows)
            obs_rows[at, :] = ring[source, which, 0].astype(F32)
            innov_rows[at, :] = ring[source, which, 1].astype(F32)
        place = geo_sel[which]
        (y1, y2, y3), norms, ones = pieces(place)
        feat_rows[0:FEATS, :] = jnp.concatenate(
            [-2.0 * y1, -2.0 * y2, -2.0 * y1, -2.0 * y2, -2.0 * y3, -2.0 * y1, ones, norms], axis=0
        )
        for part in range(panels):
            lanes = slice(part * TILE, (part + 1) * TILE)
            model = obs_rows[:, lanes]
            deviation = model - jnp.sum(model, axis=0, keepdims=True) / members
            spread = (
                jnp.sum(deviation * deviation, axis=0, keepdims=True) / (members - 1)
                + place[3:4, lanes]
            )
            panel = which * panels + part
            panel_left[panel, :, 0:members] = deviation.T.astype(BF16)
            panel_left[panel, :, TILE:] = feat_rows[:, lanes].T.astype(BF16)
            panel_weight[panel] = (innov_rows[:, lanes] * (1.0 / spread)).astype(BF16)
        return carry

    lax.fori_loop(0, 3, prepare, 0)

    scale = 1.0 / (members - 1)

    def await_chunk(chunk):
        pltpu.make_async_copy(
            arrived.at[chunk, 0 : devices - 1], arrived.at[chunk, 0 : devices - 1], in_recv.at[chunk]
        ).wait()
        pltpu.make_async_copy(arrived.at[chunk, 0], arrived.at[chunk, 0], in_own.at[chunk]).wait()

    def products(chunk, block, field, right, product):
        index = chunk * blocks + block
        lanes = slice(block * TILE, (block + 1) * TILE)
        for source in range(devices):
            field[source * rows : (source + 1) * rows, :] = arrived[chunk, source, :, lanes].astype(F32)
        value = field[...]
        centre = jnp.sum(value, axis=0, keepdims=True) / members
        right[0:members, 0:TILE] = (value - centre).astype(BF16)
        right[TILE : TILE + FEATS, TILE:] = state_feats[
            :, pl.ds(pl.multiple_of(index * TILE, TILE), TILE)
        ]
        left = jnp.concatenate([panel_left[pattern[index, slot]] for slot in range(slots)], axis=0)
        product[...] = jnp.dot(left, right[...], preferred_element_type=F32)

    def update(chunk, block, field, product):
        index = chunk * blocks + block
        live = counts[0, index]
        gains, weights = [], []
        for slot in range(slots):
            at = slice(slot * TILE, (slot + 1) * TILE)
            gains.append((taper(product[at, TILE:], scale) * product[at, 0:TILE]).astype(BF16))
            mask = jnp.where(slot < live, 1.0, 0.0).astype(F32)
            weights.append(
                panel_weight[pattern[index, slot]] * jnp.full((members, TILE), mask, F32).astype(BF16)
            )
        results[:, block * TILE : (block + 1) * TILE] = field[...] + jnp.dot(
            jnp.concatenate(weights, axis=1),
            jnp.concatenate(gains, axis=0),
            preferred_element_type=F32,
        )

    await_chunk(0)
    products(0, 0, field_a, right_a, product_a)

    def analyse_chunk(chunk, carry):
        for block in range(0, blocks, 2):
            products(chunk, block + 1, field_b, right_b, product_b)
            update(chunk, block, field_a, product_a)
            if block + 2 < blocks:
                products(chunk, block + 2, field_a, right_a, product_a)
            else:

                @pl.when(chunk + 1 < chunks)
                def _():
                    await_chunk(chunk + 1)

                coming = jnp.minimum(chunk + 1, chunks - 1)
                products(coming, 0, field_a, right_a, product_a)
            update(chunk, block + 1, field_b, product_b)
        for target in range(devices):
            leaving[chunk, target] = results[target * rows : (target + 1) * rows, :].astype(BF16)
        begin = pl.multiple_of(me * entries + chunk * width, TILE)

        def send_back(step, carry):
            peer = wrap(me + step, devices)
            pltpu.make_async_remote_copy(
                src_ref=leaving.at[chunk, peer],
                dst_ref=out.at[:, pl.ds(begin, width)],
                send_sem=out_send,
                recv_sem=out_recv,
                device_id=(my_region, peer),
                device_id_type=MESH,
            ).start()
            return carry

        lax.fori_loop(1, devices, send_back, 0)
        pltpu.make_async_copy(
            leaving.at[chunk, me], out.at[:, pl.ds(begin, width)], in_own.at[chunk]
        ).start()
        return carry

    lax.fori_loop(0, chunks, analyse_chunk, 0)

    for chunk in range(chunks):
        pltpu.make_async_copy(leaving.at[chunk, 0], leaving.at[chunk, 0], in_own.at[chunk]).wait()
    others = leaving.at[:, 0 : devices - 1]
    pltpu.make_async_copy(others, others, out_recv).wait()
    pltpu.make_async_copy(others, others, out_send).wait()
    pltpu.make_async_copy(others, others, in_send).wait()
    pltpu.make_async_copy(gathered.at[0 : regions - 1], gathered.at[0 : regions - 1], xy_send).wait()
    pltpu.make_async_copy(
        gathered_geo.at[0 : regions - 1], gathered_geo.at[0 : regions - 1], geo_send
    ).wait()
    pltpu.make_async_copy(ring.at[0:ups], ring.at[0:ups], up_send).wait()
    if downs > 0:
        pltpu.make_async_copy(ring.at[0:downs], ring.at[0:downs], down_send).wait()
    pltpu.make_async_copy(ring.at[0:chips], ring.at[0:chips], sib_send).wait()


def on_device(
    regions,
    devices,
    sample_matrix,
    state_coords,
    obs_model,
    innovations,
    obs_error,
    obs_coords,
    neighbours,
    pattern,
    counts,
):
    rows = sample_matrix.shape[0]
    obs_count = obs_model.shape[1]
    entries = state_coords.shape[1]
    width = entries // CHUNKS
    members = rows * devices
    panels = 3 * obs_count // TILE
    slots = pattern.shape[1]
    chips = devices // 2
    hbm = pl.BlockSpec(memory_space=pltpu.HBM)
    dma = pltpu.SemaphoreType.DMA
    return pl.pallas_call(
        functools.partial(kernel, (regions, devices)),
        out_shape=jax.ShapeDtypeStruct(sample_matrix.shape, sample_matrix.dtype),
        in_specs=[hbm] * 9,
        out_specs=hbm,
        scratch_shapes=[
            pltpu.VMEM((1, obs_count), F32),
            pltpu.VMEM(obs_coords.shape, F32),
            pltpu.VMEM(state_coords.shape, F32),
            pltpu.SMEM(neighbours.shape, jnp.int32),
            pltpu.SMEM(pattern.shape, jnp.int32),
            pltpu.SMEM((1, counts.shape[0]), jnp.int32),
            dma((8,)),
            pltpu.VMEM((2, rows, obs_count), BF16),
            pltpu.VMEM((4, obs_count), F32),
            pltpu.VMEM((regions, 2, rows, obs_count), BF16),
            pltpu.VMEM((regions, 4, obs_count), F32),
            pltpu.VMEM((devices, 3, 2, rows, obs_count), BF16),
            pltpu.VMEM((3, 4, obs_count), F32),
            pltpu.VMEM((CHUNKS, devices, rows, width), BF16),
            pltpu.VMEM((members, TILE), F32),
            pltpu.VMEM((members, TILE), F32),
            pltpu.VMEM((members, width), F32),
            pltpu.VMEM((CHUNKS, devices, rows, width), BF16),
            pltpu.VMEM((members, obs_count), F32),
            pltpu.VMEM((members, obs_count), F32),
            pltpu.VMEM((TILE, obs_count), F32),
            pltpu.VMEM((FEATS, entries), BF16),
            pltpu.VMEM((panels, TILE, 2 * TILE), BF16),
            pltpu.VMEM((panels, members, TILE), BF16),
            pltpu.VMEM((2 * TILE, 2 * TILE), BF16),
            pltpu.VMEM((2 * TILE, 2 * TILE), BF16),
            pltpu.VMEM((slots * TILE, 2 * TILE), F32),
            pltpu.VMEM((slots * TILE, 2 * TILE), F32),
            dma,
            dma,
            dma,
            dma,
            dma,
            dma((2, chips)),
            dma,
            dma((2, chips)),
            dma,
            dma,
            dma,
            dma((CHUNKS,)),
            dma((CHUNKS,)),
            dma,
            dma,
        ],
        compiler_params=pltpu.CompilerParams(
            collective_id=0, has_side_effects=True, vmem_limit_bytes=60 * 2**20
        ),
    )(
        sample_matrix,
        obs_model,
        innovations,
        obs_error.reshape(1, -1),
        obs_coords,
        state_coords,
        neighbours,
        pattern,
        counts.reshape(1, -1),
    )


def solution(mesh):
    in_specs = (
        P("member", "region"),
        P(None, ("region", "member")),
        P("member", "region"),
        P("member", "region"),
        P("region"),
        P(None, "region"),
        P("region", None),
        P(("region", "member"), None),
        P(("region", "member")),
    )
    return jax.shard_map(
        functools.partial(on_device, mesh.shape["region"], mesh.shape["member"]),
        mesh=mesh,
        in_specs=in_specs,
        out_specs=P("member", "region"),
        check_vma=False,
    )
```
